32 devices in a mesh: dp: 16 (over z, x, core), feat: 2 (over y).
Axes of the slice: x: 2, y: 2, z: 4, core: 2. Of those that a mesh axis runs over, the one named last changes fastest.
Arguments:
- proj_grads: bfloat16 [4096, 16384], P('dp', 'feat'), may hold values from -1.25 to 1.25
- val_grads: bfloat16 [16384, 128], P('feat'), may hold values from -1.25 to 1.25
Outputs:
- interactions: bfloat16 [4096, 4096], P('dp', 'feat')
- data_scores: float32 [4096, 128], P('dp')
The draws below stay inside these ranges and needn't reach their ends.
All inputs are finite; a program needn't handle non-finite values.
Results may differ from the reference program's by a relative error of at most 0.0006.
Values may be sent and summed in bfloat16 or wider, within the bound.
A program may use at most 192 MiB of HBM per device.

```python
import jax
import jax.numpy as jnp
from jax import lax

K = 16384
ROWS = 256
Q = 128
EXAMPLES = 4096
N_DP = 16


def block_levels(key, shape, pieces, least, top_value):
    def one(dim, shards_of):
        heights = jax.random.uniform(jax.random.fold_in(jax.random.fold_in(key, 6), dim), (shards_of,), jnp.float32, least / len(pieces), top_value / len(pieces))
        return jnp.repeat(jnp.exp(heights), shape[dim] // shards_of).reshape((-1,) + (1,) * (len(shape) - dim - 1))

    factor_of = one(*pieces[0])
    for cut in pieces[1:]:
        factor_of = factor_of * one(*cut)
    return factor_of


def gaussian(stream_key, shape, width, bound, cuts=(), held_as=jnp.bfloat16):
    array = width * jax.random.normal(stream_key, shape, jnp.float32)
    if cuts:
        array = array * block_levels(stream_key, shape, cuts, -0.22, 0.18)
    return jnp.clip(array, -bound, bound).astype(held_as)


def setup_inputs(seed: int = 0) -> dict:
    streams_of = jax.random.split(jax.random.key(seed), 3)
    proj_grads = gaussian(streams_of[0], (EXAMPLES, K), 0.0884, 1.25, ((0, 16), (1, 2)))
    val_grads = gaussian(streams_of[1], (K, Q), 0.0884, 1.25, ((0, 2),))
    return dict(proj_grads=proj_grads, val_grads=val_grads)


def reference(proj_grads, val_grads):
    pair_weight = 1.0 / (ROWS ** 0.5)
    first = jnp.dot(proj_grads, val_grads, preferred_element_type=jnp.float32)
    blocks = proj_grads.reshape(N_DP, ROWS, K)
    bases = jnp.arange(N_DP, dtype=jnp.int32) * ROWS
    col_index = jnp.arange(ROWS * N_DP, dtype=jnp.int32)

    def one_block(inputs):
        block, base = inputs
        gram_rows = jnp.dot(block, proj_grads.T, preferred_element_type=jnp.float32)
        row_index = base + jnp.arange(ROWS, dtype=jnp.int32)
        pair_values = jnp.where(row_index[:, None] == col_index[None, :], 0.0, gram_rows)
        pair_sum = jnp.dot(pair_values, first, precision=lax.Precision.HIGHEST)
        return pair_values.astype(jnp.bfloat16), pair_sum

    inter_blocks, sum_blocks = lax.map(one_block, (blocks, bases))
    interactions = inter_blocks.reshape(ROWS * N_DP, ROWS * N_DP)
    pair_sum = sum_blocks.reshape(ROWS * N_DP, first.shape[1])
    return interactions, first - pair_weight * pair_sum
```

```python
import functools

import jax
import jax.numpy as jnp
from jax import lax
from jax.sharding import PartitionSpec as P


def pair_tile(left_rows, right_rows):
    return lax.dot_general(
        left_rows, right_rows, (((1,), (1,)), ((), ())), preferred_element_type=jnp.float32
    )


def general_body(proj_grads, val_grads):
    row_count = proj_grads.shape[0]
    pair_weight = 1.0 / row_count**0.5
    dp_index = lax.axis_index("dp")
    feat_index = lax.axis_index("feat")
    first_local = lax.psum(
        jnp.dot(proj_grads, val_grads, preferred_element_type=jnp.float32), "feat"
    )
    block_row = pair_tile(proj_grads, lax.all_gather(proj_grads, "dp", axis=0, tiled=True))
    gram_cols = lax.psum_scatter(block_row, "feat", scatter_dimension=1, tiled=True)
    col_count = gram_cols.shape[1]
    row_ids = dp_index * row_count + jnp.arange(row_count, dtype=jnp.int32)
    col_ids = feat_index * col_count + jnp.arange(col_count, dtype=jnp.int32)
    pair_values = jnp.where(row_ids[:, None] == col_ids[None, :], 0.0, gram_cols)
    first_all = lax.all_gather(first_local, "dp", axis=0, tiled=True)
    first_cols = lax.dynamic_slice_in_dim(first_all, feat_index * col_count, col_count, 0)
    partial_sum = jnp.dot(pair_values, first_cols, precision=lax.Precision.HIGHEST)
    pair_sum = lax.psum(partial_sum, "feat")
    data_scores = first_local - pair_weight * pair_sum
    return (pair_values.astype(jnp.bfloat16), data_scores)


KEPT = ((0, 1), (2, 3), (1, 0), (2, 3))


def split_body(n_dp, proj_grads, val_grads):
    per_part = n_dp // 4
    half = n_dp // 2
    row_count = proj_grads.shape[0]
    pair_weight = 1.0 / row_count**0.5
    dp_index = lax.axis_index("dp")
    feat_index = lax.axis_index("feat")
    part = dp_index // per_part
    inner = dp_index % per_part
    both = ("dp", "feat")

    def flat(part, inner, feat):
        return (part * per_part + inner) * 2 + feat

    def fetch(which):
        return [
            (flat(KEPT[p][feat ^ which], i, feat), flat(p, i, feat))
            for p in (1, 2) for i in range(per_part) for feat in (0, 1)
        ]

    def deliver(flip):
        return [
            (flat(p, i, feat), flat(KEPT[p][feat], i, (p // 2) ^ flip))
            for p in range(4) for i in range(per_part) for feat in (0, 1)
        ]

    feat_swap = [(0, 1), (1, 0)]
    halves = [list(range(half)), list(range(half, n_dp))]

    far_give = lax.ppermute(proj_grads, both, fetch(1))
    far_keep = lax.ppermute(proj_grads, both, fetch(0))
    half_rows = lax.all_gather(
        proj_grads, "dp", axis=0, tiled=True, axis_index_groups=halves
    )
    first_part = jnp.dot(proj_grads, val_grads, preferred_element_type=jnp.float32)
    first_local = first_part + lax.ppermute(first_part, "feat", feat_swap)
    first_half = lax.all_gather(
        first_local, "dp", axis=0, tiled=True, axis_index_groups=halves
    )

    kept = jnp.asarray(KEPT, jnp.int32)
    keep_part = kept[part, feat_index]
    give_part = kept[part, 1 - feat_index]
    is_inner = (part == 1) | (part == 2)

    def near(which_part):
        start = ((which_part % 2) * per_part + inner) * row_count
        return lax.dynamic_slice_in_dim(half_rows, start, row_count, 0)

    give_rows = jnp.where(is_inner, far_give, near(give_part))
    given = lax.ppermute(pair_tile(give_rows, half_rows), "feat", feat_swap)
    keep_rows = jnp.where(is_inner, far_keep, near(keep_part))
    gram_cols = pair_tile(keep_rows, half_rows) + given
    col_count = gram_cols.shape[1]
    row_ids = (keep_part * per_part + inner) * row_count + jnp.arange(row_count, dtype=jnp.int32)
    col_ids = (part // 2) * col_count + jnp.arange(col_count, dtype=jnp.int32)
    pair_values = jnp.where(row_ids[:, None] == col_ids[None, :], 0.0, gram_cols)
    interactions = lax.ppermute(pair_values.astype(jnp.bfloat16), both, deliver(0))
    partial_sum = jnp.dot(pair_values, first_half, precision=lax.Precision.HIGHEST)
    pair_sum = lax.ppermute(partial_sum, both, deliver(0)) + lax.ppermute(
        partial_sum, both, deliver(1)
    )
    return (interactions, first_local - pair_weight * pair_sum)


def solution(mesh):
    n_dp = mesh.shape["dp"]
    if mesh.shape["feat"] == 2 and n_dp % 4 == 0:
        body = functools.partial(split_body, n_dp)
    else:
        body = general_body
    return jax.shard_map(
        body,
        mesh=mesh,
        in_specs=(P("dp", "feat"), P("feat", None)),
        out_specs=(P("dp", "feat"), P("dp", None)),
        check_vma=False,
    )
```

```python
import jax
import jax.numpy as jnp
from jax import lax
from jax.sharding import PartitionSpec as P


def pair_tile(left_rows, right_rows):
    return lax.dot_general(
        left_rows, right_rows, (((1,), (1,)), ((), ())), preferred_element_type=jnp.float32
    )


def general_body(proj_grads, val_grads):
    row_count = proj_grads.shape[0]
    pair_weight = 1.0 / row_count**0.5
    dp_index = lax.axis_index("dp")
    feat_index = lax.axis_index("feat")
    first_local = lax.psum(
        jnp.dot(proj_grads, val_grads, preferred_element_type=jnp.float32), "feat"
    )
    block_row = pair_tile(proj_grads, lax.all_gather(proj_grads, "dp", axis=0, tiled=True))
    gram_cols = lax.psum_scatter(block_row, "feat", scatter_dimension=1, tiled=True)
    col_count = gram_cols.shape[1]
    row_ids = dp_index * row_count + jnp.arange(row_count, dtype=jnp.int32)
    col_ids = feat_index * col_count + jnp.arange(col_count, dtype=jnp.int32)
    pair_values = jnp.where(row_ids[:, None] == col_ids[None, :], 0.0, gram_cols)
    first_all = lax.all_gather(first_local, "dp", axis=0, tiled=True)
    first_cols = lax.dynamic_slice_in_dim(first_all, feat_index * col_count, col_count, 0)
    partial_sum = jnp.dot(pair_values, first_cols, precision=lax.Precision.HIGHEST)
    pair_sum = lax.psum(partial_sum, "feat")
    data_scores = first_local - pair_weight * pair_sum
    return (pair_values.astype(jnp.bfloat16), data_scores)


ROWS_OF = ((0, 1), (2, 3), (1, 0), (3, 2))


def split_body(proj_grads, val_grads):
    row_count, width = proj_grads.shape
    pair_weight = 1.0 / row_count**0.5
    dp_index = lax.axis_index("dp")
    feat_index = lax.axis_index("feat")
    part, side, core = dp_index // 4, dp_index // 2 % 2, dp_index % 2
    is_inner = (part == 1) | (part == 2)
    both = ("dp", "feat")

    def at(part, side, core):
        return (part * 2 + side) * 2 + core

    def moves(to, parts=range(4)):
        return [
            (at(p, s, c), at(*to(p, s, c))) for p in parts for s in (0, 1) for c in (0, 1)
        ]

    core_swap = moves(lambda p, s, c: (p, s, 1 - c))
    side_swap = moves(lambda p, s, c: (p, 1 - s, c))
    part_swap = moves(lambda p, s, c: (p ^ 1, s, c))
    near_swap = moves(lambda p, s, c: (3 - p, s, c), (1, 2))
    far_move = moves(lambda p, s, c: (2 if p == 0 else 1, s, c), (0, 3))
    feat_swap = [(0, 1), (1, 0)]

    def ordered(flag, mine, other, axis):
        low = jnp.where(flag == 0, mine, other)
        high = jnp.where(flag == 0, other, mine)
        return jnp.concatenate([low, high], axis)

    half_width = width // 2
    mine = lax.dynamic_slice_in_dim(proj_grads, core * half_width, half_width, 1)
    give = lax.dynamic_slice_in_dim(proj_grads, (1 - core) * half_width, half_width, 1)
    own = ordered(core, mine, lax.ppermute(give, "dp", core_swap), 0)

    by_part = lax.ppermute(own, "dp", part_swap)
    by_side = lax.ppermute(own, "dp", side_swap)
    near = lax.ppermute(own, "dp", near_swap)
    first_part = jnp.dot(proj_grads, val_grads, preferred_element_type=jnp.float32)
    first_local = first_part + lax.ppermute(first_part, "feat", feat_swap)

    own_late, by_part_late, first_local = lax.optimization_barrier((own, by_part, first_local))
    far = lax.ppermute(own_late, "dp", far_move)
    by_both = lax.ppermute(by_part_late, "dp", side_swap)
    half = lax.axis_size("dp") // 2
    first_half = lax.all_gather(
        first_local, "dp", axis=0, tiled=True,
        axis_index_groups=[list(range(half)), list(range(half, 2 * half))],
    )

    def summed(tile):
        rows = tile.shape[0] // 2
        keep = lax.dynamic_slice_in_dim(tile, core * rows, rows, 0)
        send = lax.dynamic_slice_in_dim(tile, (1 - core) * rows, rows, 0)
        tile = keep + lax.ppermute(send, "dp", core_swap)
        rows = rows // 2
        keep = lax.dynamic_slice_in_dim(tile, feat_index * rows, rows, 0)
        send = lax.dynamic_slice_in_dim(tile, (1 - feat_index) * rows, rows, 0)
        return keep + lax.ppermute(send, "feat", feat_swap)

    rows_a = jnp.where(is_inner, near, own)
    early = summed(
        jnp.concatenate([pair_tile(rows_a, cols) for cols in (own, by_side, by_part)], 1)
    )
    far, by_both, early, first_half = lax.optimization_barrier((far, by_both, early, first_half))
    rows_b = jnp.where(is_inner, far, by_part)
    late_b = summed(
        jnp.concatenate([pair_tile(rows_b, cols) for cols in (own, by_side, by_part, by_both)], 1)
    )
    late_a = summed(pair_tile(rows_a, by_both))
    gram = jnp.concatenate([jnp.concatenate([early, late_a], 1), late_b], 0)

    chip_cols = own.shape[0]
    own_x, side_x, part_x, both_x = (
        gram[:, i * chip_cols:(i + 1) * chip_cols] for i in range(4)
    )
    gram_cols = ordered(
        part % 2,
        ordered(side, own_x, side_x, 1),
        ordered(side, part_x, both_x, 1),
        1,
    )
    rows_of = jnp.asarray(ROWS_OF, jnp.int32)[part]
    piece = row_count // 2
    row_base = ((rows_of * 2 + side) * 2 + core) * row_count + feat_index * piece
    row_ids = (row_base[:, None] + jnp.arange(piece, dtype=jnp.int32)[None, :]).reshape(-1)
    col_count = gram_cols.shape[1]
    col_ids = (part // 2) * col_count + jnp.arange(col_count, dtype=jnp.int32)
    pair_values = jnp.where(row_ids[:, None] == col_ids[None, :], 0.0, gram_cols)
    partial_sum = jnp.dot(pair_values, first_half, precision=lax.Precision.HIGHEST)

    def deliver(values):
        out = []
        for flip in (0, 1):
            sent = jnp.where((feat_index ^ flip) == 0, values[:piece], values[piece:])
            out.append(lax.ppermute(sent, both, [
                (at(p, s, c) * 2 + f, at(ROWS_OF[p][f ^ flip], s, c) * 2 + p // 2)
                for p in range(4) for s in (0, 1) for c in (0, 1) for f in (0, 1)
            ]))
        return ordered((part + feat_index) % 2, out[0], out[1], 0)

    half_sum = deliver(partial_sum)
    interactions = deliver(pair_values.astype(jnp.bfloat16))
    pair_sum = half_sum + lax.ppermute(half_sum, "feat", feat_swap)
    return (interactions, first_local - pair_weight * pair_sum)


def solution(mesh):
    split = mesh.shape["feat"] == 2 and mesh.shape["dp"] == 16
    return jax.shard_map(
        split_body if split else general_body,
        mesh=mesh,
        in_specs=(P("dp", "feat"), P("feat", None)),
        out_specs=(P("dp", "feat"), P("dp", None)),
        check_vma=False,
    )
```

```python
import jax
import jax.numpy as jnp
from jax import lax
from jax.sharding import PartitionSpec as P


def pair_tile(left_rows, right_rows):
    return lax.dot_general(
        left_rows, right_rows, (((1,), (1,)), ((), ())), preferred_element_type=jnp.float32
    )


def general_body(proj_grads, val_grads):
    row_count = proj_grads.shape[0]
    pair_weight = 1.0 / row_count**0.5
    dp_index = lax.axis_index("dp")
    feat_index = lax.axis_index("feat")
    first_local = lax.psum(
        jnp.dot(proj_grads, val_grads, preferred_element_type=jnp.float32), "feat"
    )
    block_row = pair_tile(proj_grads, lax.all_gather(proj_grads, "dp", axis=0, tiled=True))
    gram_cols = lax.psum_scatter(block_row, "feat", scatter_dimension=1, tiled=True)
    col_count = gram_cols.shape[1]
    row_ids = dp_index * row_count + jnp.arange(row_count, dtype=jnp.int32)
    col_ids = feat_index * col_count + jnp.arange(col_count, dtype=jnp.int32)
    pair_values = jnp.where(row_ids[:, None] == col_ids[None, :], 0.0, gram_cols)
    first_all = lax.all_gather(first_local, "dp", axis=0, tiled=True)
    first_cols = lax.dynamic_slice_in_dim(first_all, feat_index * col_count, col_count, 0)
    partial_sum = jnp.dot(pair_values, first_cols, precision=lax.Precision.HIGHEST)
    pair_sum = lax.psum(partial_sum, "feat")
    data_scores = first_local - pair_weight * pair_sum
    return (pair_values.astype(jnp.bfloat16), data_scores)


ROWS_OF = ((0, 1), (2, 3), (1, 0), (3, 2))


def split_body(proj_grads, val_grads):
    row_count, width = proj_grads.shape
    pair_weight = 1.0 / row_count**0.5
    dp_index = lax.axis_index("dp")
    feat_index = lax.axis_index("feat")
    part, side, core = dp_index // 4, dp_index // 2 % 2, dp_index % 2
    is_inner = (part == 1) | (part == 2)
    both = ("dp", "feat")

    def at(part, side, core):
        return (part * 2 + side) * 2 + core

    def moves(to, parts=range(4)):
        return [
            (at(p, s, c), at(*to(p, s, c))) for p in parts for s in (0, 1) for c in (0, 1)
        ]

    core_swap = moves(lambda p, s, c: (p, s, 1 - c))
    side_swap = moves(lambda p, s, c: (p, 1 - s, c))
    part_swap = moves(lambda p, s, c: (p ^ 1, s, c))
    near_swap = moves(lambda p, s, c: (3 - p, s, c), (1, 2))
    far_move = moves(lambda p, s, c: (2 if p == 0 else 1, s, c), (0, 3))
    feat_swap = [(0, 1), (1, 0)]

    def ordered(flag, mine, other, axis):
        low = jnp.where(flag == 0, mine, other)
        high = jnp.where(flag == 0, other, mine)
        return jnp.concatenate([low, high], axis)

    half_width, piece = width // 2, row_count // 2
    mine = lax.dynamic_slice_in_dim(proj_grads, core * half_width, half_width, 1)
    give = lax.dynamic_slice_in_dim(proj_grads, (1 - core) * half_width, half_width, 1)
    other = lax.ppermute(give, "dp", core_swap)
    own = [ordered(core, mine[:piece], other[:piece], 0), ordered(core, mine[piece:], other[piece:], 0)]

    by_part = [lax.ppermute(rows, "dp", part_swap) for rows in own]
    by_side = [lax.ppermute(rows, "dp", side_swap) for rows in own]
    near = [lax.ppermute(rows, "dp", near_swap) for rows in own]
    first_part = jnp.dot(proj_grads, val_grads, preferred_element_type=jnp.float32)
    first_local = first_part + lax.ppermute(first_part, "feat", feat_swap)

    far_0, by_both_0, far_1, by_both_1, first_local = lax.optimization_barrier(
        (own[0], by_part[0], own[1], by_part[1], first_local)
    )
    far_0 = lax.ppermute(far_0, "dp", far_move)
    by_both_0 = lax.ppermute(by_both_0, "dp", side_swap)
    half = lax.axis_size("dp") // 2
    first_half = lax.all_gather(
        first_local, "dp", axis=0, tiled=True,
        axis_index_groups=[list(range(half)), list(range(half, 2 * half))],
    )

    def summed(rows, cols):
        tile = jnp.concatenate(
            [jnp.concatenate([pair_tile(r, c) for c in cols], 1) for r in rows], 0
        )
        tile = tile.reshape(len(rows), 2, piece, tile.shape[1])
        keep = lax.dynamic_index_in_dim(tile, core, 1, False)
        send = lax.dynamic_index_in_dim(tile, 1 - core, 1, False)
        tile = keep + lax.ppermute(send, "dp", core_swap)
        tile = tile.reshape(len(rows), 2, piece // 2, tile.shape[2])
        keep = lax.dynamic_index_in_dim(tile, feat_index, 1, False)
        send = lax.dynamic_index_in_dim(tile, 1 - feat_index, 1, False)
        tile = keep + lax.ppermute(send, "feat", feat_swap)
        return tile.reshape(-1, tile.shape[2])

    rows_a = [jnp.where(is_inner, n, o) for n, o in zip(near, own)]
    cols = own + by_side + by_part
    gram_a = summed(rows_a, cols)
    far_0, by_both_0, far_1, by_both_1 = lax.optimization_barrier(
        (far_0, by_both_0, far_1, by_both_1)
    )
    far_1 = lax.ppermute(far_1, "dp", far_move)
    by_both_1 = lax.ppermute(by_both_1, "dp", side_swap)
    rows_b0 = jnp.where(is_inner, far_0, by_part[0])
    gram_b0 = summed([rows_b0], cols)
    gram_c0 = summed(rows_a + [rows_b0], [by_both_0])
    far_1, by_both_1, gram_a, gram_b0, gram_c0, first_half = lax.optimization_barrier(
        (far_1, by_both_1, gram_a, gram_b0, gram_c0, first_half)
    )
    gram_c1 = summed(rows_a + [rows_b0], [by_both_1])
    rows_b1 = jnp.where(is_inner, far_1, by_part[1])
    gram_b1 = summed([rows_b1], cols + [by_both_0, by_both_1])

    rows_of = jnp.asarray(ROWS_OF, jnp.int32)[part]
    offsets = jnp.concatenate(
        [c * piece + feat_index * (piece // 2) + jnp.arange(piece // 2, dtype=jnp.int32) for c in (0, 1)]
    )

    def finished(tile, which):
        col_count = tile.shape[1]
        block = piece
        chips = []
        for chip in range(4):
            part_of = [
                tile[:, (chip * 4 + k) * block:(chip * 4 + k + 1) * block] for k in (0, 2, 1, 3)
            ]
            chips.append(jnp.concatenate(part_of, 1))
        tile = ordered(
            part % 2, ordered(side, chips[0], chips[1], 1), ordered(side, chips[2], chips[3], 1), 1
        )
        row_ids = ((rows_of[which] * 2 + side) * 2 + core) * row_count + offsets
        col_ids = (part // 2) * col_count + jnp.arange(col_count, dtype=jnp.int32)
        values = jnp.where(row_ids[:, None] == col_ids[None, :], 0.0, tile)
        return values, jnp.dot(values, first_half, precision=lax.Precision.HIGHEST)

    def deliver(values, which):
        return [
            lax.ppermute(values, both, [
                (at(p, s, c) * 2 + f, at(ROWS_OF[p][which], s, c) * 2 + p // 2)
                for p in range(4) for s in (0, 1) for c in (0, 1)
            ])
            for f in (0, 1)
        ]

    def placed(from_a, from_b):
        takes_a = (part + feat_index) % 2 == 0
        low, high = (jnp.where(takes_a, a, b) for a, b in zip(from_a, from_b))
        rows = piece // 2
        return jnp.concatenate([low[:rows], high[:rows], low[rows:], high[rows:]], 0)

    kept = gram_c0.shape[0] * 2 // 3
    values_a, sums_a = finished(jnp.concatenate([gram_a, gram_c0[:kept], gram_c1[:kept]], 1), 0)
    sent_a = deliver(values_a.astype(jnp.bfloat16), 0)
    sent_sums_a = deliver(sums_a, 0)
    rows_0 = jnp.concatenate([gram_b0, gram_c0[kept:], gram_c1[kept:]], 1)
    values_b, sums_b = finished(jnp.concatenate([rows_0, gram_b1], 0), 1)
    half_sum = placed(sent_sums_a, deliver(sums_b, 1))
    interactions = placed(sent_a, deliver(values_b.astype(jnp.bfloat16), 1))
    pair_sum = half_sum + lax.ppermute(half_sum, "feat", feat_swap)
    return (interactions, first_local - pair_weight * pair_sum)


def solution(mesh):
    split = mesh.shape["feat"] == 2 and mesh.shape["dp"] == 16
    return jax.shard_map(
        split_body if split else general_body,
        mesh=mesh,
        in_specs=(P("dp", "feat"), P("feat", None)),
        out_specs=(P("dp", "feat"), P("dp", None)),
        check_vma=False,
    )
```

```python
import jax
import jax.numpy as jnp
from jax import lax
from jax.sharding import PartitionSpec as P


def pair_tile(left_rows, right_rows):
    return lax.dot_general(
        left_rows, right_rows, (((1,), (1,)), ((), ())), preferred_element_type=jnp.float32
    )


def general_body(proj_grads, val_grads):
    row_count = proj_grads.shape[0]
    pair_weight = 1.0 / row_count**0.5
    dp_index = lax.axis_index("dp")
    feat_index = lax.axis_index("feat")
    first_local = lax.psum(
        jnp.dot(proj_grads, val_grads, preferred_element_type=jnp.float32), "feat"
    )
    block_row = pair_tile(proj_grads, lax.all_gather(proj_grads, "dp", axis=0, tiled=True))
    gram_cols = lax.psum_scatter(block_row, "feat", scatter_dimension=1, tiled=True)
    col_count = gram_cols.shape[1]
    row_ids = dp_index * row_count + jnp.arange(row_count, dtype=jnp.int32)
    col_ids = feat_index * col_count + jnp.arange(col_count, dtype=jnp.int32)
    pair_values = jnp.where(row_ids[:, None] == col_ids[None, :], 0.0, gram_cols)
    first_all = lax.all_gather(first_local, "dp", axis=0, tiled=True)
    first_cols = lax.dynamic_slice_in_dim(first_all, feat_index * col_count, col_count, 0)
    partial_sum = jnp.dot(pair_values, first_cols, precision=lax.Precision.HIGHEST)
    pair_sum = lax.psum(partial_sum, "feat")
    data_scores = first_local - pair_weight * pair_sum
    return (pair_values.astype(jnp.bfloat16), data_scores)


ROWS_OF = ((0, 1), (2, 3), (1, 0), (3, 2))


def split_body(proj_grads, val_grads):
    row_count, width = proj_grads.shape
    pair_weight = 1.0 / row_count**0.5
    dp_index = lax.axis_index("dp")
    feat_index = lax.axis_index("feat")
    part, side, core = dp_index // 4, dp_index // 2 % 2, dp_index % 2
    is_inner = (part == 1) | (part == 2)
    both = ("dp", "feat")

    def at(part, side, core):
        return (part * 2 + side) * 2 + core

    def moves(to, parts=range(4)):
        return [
            (at(p, s, c), at(*to(p, s, c))) for p in parts for s in (0, 1) for c in (0, 1)
        ]

    core_swap = moves(lambda p, s, c: (p, s, 1 - c))
    side_swap = moves(lambda p, s, c: (p, 1 - s, c))
    part_swap = moves(lambda p, s, c: (p ^ 1, s, c))
    near_swap = moves(lambda p, s, c: (3 - p, s, c), (1, 2))
    far_move = moves(lambda p, s, c: (2 if p == 0 else 1, s, c), (0, 3))
    feat_swap = [(0, 1), (1, 0)]

    def ordered(flag, mine, other, axis):
        low = jnp.where(flag == 0, mine, other)
        high = jnp.where(flag == 0, other, mine)
        return jnp.concatenate([low, high], axis)

    half_width = width // 2
    mine = lax.dynamic_slice_in_dim(proj_grads, core * half_width, half_width, 1)
    give = lax.dynamic_slice_in_dim(proj_grads, (1 - core) * half_width, half_width, 1)
    own = ordered(core, mine, lax.ppermute(give, "dp", core_swap), 0)

    by_part = lax.ppermute(own, "dp", part_swap)
    by_side = lax.ppermute(own, "dp", side_swap)
    near = lax.ppermute(own, "dp", near_swap)
    first_part = jnp.dot(proj_grads, val_grads, preferred_element_type=jnp.float32)
    first_local = first_part + lax.ppermute(first_part, "feat", feat_swap)

    own_late, by_part_late, first_local = lax.optimization_barrier((own, by_part, first_local))
    far = lax.ppermute(own_late, "dp", far_move)
    by_both = lax.ppermute(by_part_late, "dp", side_swap)
    half = lax.axis_size("dp") // 2
    first_half = lax.all_gather(
        first_local, "dp", axis=0, tiled=True,
        axis_index_groups=[list(range(half)), list(range(half, 2 * half))],
    )

    def shared(tile, index, name, swap):
        rows = tile.shape[0] // 2
        keep = lax.dynamic_slice_in_dim(tile, index * rows, rows, 0)
        send = lax.dynamic_slice_in_dim(tile, (1 - index) * rows, rows, 0)
        return keep + lax.ppermute(send, name, swap)

    def core_sum(tile):
        return shared(tile, core, "dp", core_swap)

    def feat_sum(tile):
        return shared(tile, feat_index, "feat", feat_swap)

    def products(rows, chips):
        return jnp.concatenate([pair_tile(rows, cols) for cols in chips], 1)

    rows_a = jnp.where(is_inner, near, own)
    early = feat_sum(core_sum(products(rows_a, (own, by_side, by_part))))
    far, by_both, early, first_half = lax.optimization_barrier((far, by_both, early, first_half))
    rows_b = jnp.where(is_inner, far, by_part)
    b_low = core_sum(products(rows_b, (own, by_side)))
    late_a = feat_sum(core_sum(pair_tile(rows_a, by_both)))
    b_low, by_part_late, by_both_late = lax.optimization_barrier((b_low, by_part, by_both))
    b_high = core_sum(products(rows_b, (by_part_late, by_both_late)))
    late_b = [feat_sum(b_low), feat_sum(b_high)]

    rows_of = jnp.asarray(ROWS_OF, jnp.int32)[part]
    piece = row_count // 2

    def finished(tile, which):
        col_count = tile.shape[1]
        chip_cols = own.shape[0]
        own_x, side_x, part_x, both_x = (
            tile[:, i * chip_cols:(i + 1) * chip_cols] for i in range(4)
        )
        tile = ordered(
            part % 2, ordered(side, own_x, side_x, 1), ordered(side, part_x, both_x, 1), 1
        )
        row_base = ((rows_of[which] * 2 + side) * 2 + core) * row_count + feat_index * piece
        row_ids = row_base + jnp.arange(piece, dtype=jnp.int32)
        col_ids = (part // 2) * col_count + jnp.arange(col_count, dtype=jnp.int32)
        return jnp.where(row_ids[:, None] == col_ids[None, :], 0.0, tile)

    def weighted(values):
        return jnp.dot(values, first_half, precision=lax.Precision.HIGHEST)

    def deliver(values, which):
        return [
            lax.ppermute(values, both, [
                (at(p, s, c) * 2 + f, at(ROWS_OF[p][which], s, c) * 2 + p // 2)
                for p in range(4) for s in (0, 1) for c in (0, 1)
            ])
            for f in (0, 1)
        ]

    takes_a = (part + feat_index) % 2 == 0

    def placed(from_a, from_b):
        return jnp.concatenate([jnp.where(takes_a, a, b) for a, b in zip(from_a, from_b)], 0)

    values_a = finished(jnp.concatenate([early, late_a], 1), 0)
    sent_a = deliver(values_a.astype(jnp.bfloat16), 0)
    sent_sums_a = deliver(weighted(values_a), 0)
    sent_a, sent_sums_a, late_b = lax.optimization_barrier((sent_a, sent_sums_a, late_b))
    values_b = finished(jnp.concatenate(late_b, 1), 1)
    half_sum = placed(sent_sums_a, deliver(weighted(values_b), 1))
    interactions = placed(sent_a, deliver(values_b.astype(jnp.bfloat16), 1))
    pair_sum = half_sum + lax.ppermute(half_sum, "feat", feat_swap)
    return (interactions, first_local - pair_weight * pair_sum)


def solution(mesh):
    split = mesh.shape["feat"] == 2 and mesh.shape["dp"] == 16
    return jax.shard_map(
        split_body if split else general_body,
        mesh=mesh,
        in_specs=(P("dp", "feat"), P("feat", None)),
        out_specs=(P("dp", "feat"), P("dp", None)),
        check_vma=False,
    )
```

```python
import jax
import jax.numpy as jnp
from jax import lax
from jax.sharding import PartitionSpec as P


def pair_tile(left_rows, right_rows):
    return lax.dot_general(
        left_rows, right_rows, (((1,), (1,)), ((), ())), preferred_element_type=jnp.float32
    )


def general_body(proj_grads, val_grads):
    row_count = proj_grads.shape[0]
    pair_weight = 1.0 / row_count**0.5
    dp_index = lax.axis_index("dp")
    feat_index = lax.axis_index("feat")
    first_local = lax.psum(
        jnp.dot(proj_grads, val_grads, preferred_element_type=jnp.float32), "feat"
    )
    block_row = pair_tile(proj_grads, lax.all_gather(proj_grads, "dp", axis=0, tiled=True))
    gram_cols = lax.psum_scatter(block_row, "feat", scatter_dimension=1, tiled=True)
    col_count = gram_cols.shape[1]
    row_ids = dp_index * row_count + jnp.arange(row_count, dtype=jnp.int32)
    col_ids = feat_index * col_count + jnp.arange(col_count, dtype=jnp.int32)
    pair_values = jnp.where(row_ids[:, None] == col_ids[None, :], 0.0, gram_cols)
    first_all = lax.all_gather(first_local, "dp", axis=0, tiled=True)
    first_cols = lax.dynamic_slice_in_dim(first_all, feat_index * col_count, col_count, 0)
    rounded, pair_values = lax.optimization_barrier(
        (pair_values.astype(jnp.bfloat16), pair_values)
    )
    partial_sum = jnp.dot(pair_values, first_cols, precision=lax.Precision.HIGHEST)
    pair_sum = lax.psum(partial_sum, "feat")
    data_scores = first_local - pair_weight * pair_sum
    return (pair_values.astype(jnp.bfloat16), data_scores)


ROWS_OF = ((0, 1), (2, 3), (1, 0), (3, 2))


def split_body(proj_grads, val_grads):
    row_count, width = proj_grads.shape
    pair_weight = 1.0 / row_count**0.5
    dp_index = lax.axis_index("dp")
    feat_index = lax.axis_index("feat")
    part, side, core = dp_index // 4, dp_index // 2 % 2, dp_index % 2
    is_inner = (part == 1) | (part == 2)
    both = ("dp", "feat")

    def at(part, side, core):
        return (part * 2 + side) * 2 + core

    def moves(to, parts=range(4)):
        return [
            (at(p, s, c), at(*to(p, s, c))) for p in parts for s in (0, 1) for c in (0, 1)
        ]

    core_swap = moves(lambda p, s, c: (p, s, 1 - c))
    side_swap = moves(lambda p, s, c: (p, 1 - s, c))
    part_swap = moves(lambda p, s, c: (p ^ 1, s, c))
    near_swap = moves(lambda p, s, c: (3 - p, s, c), (1, 2))
    far_move = moves(lambda p, s, c: (2 if p == 0 else 1, s, c), (0, 3))
    feat_swap = [(0, 1), (1, 0)]

    def ordered(flag, mine, other, axis):
        if axis == 0:
            first = (jnp.arange(2, dtype=jnp.int32) == flag)[:, None, None]
            return jnp.where(first, mine[None], other[None]).reshape(-1, mine.shape[1])
        low = jnp.where(flag == 0, mine, other)
        high = jnp.where(flag == 0, other, mine)
        return jnp.concatenate([low, high], axis)

    half_width = width // 2
    mine = lax.dynamic_slice_in_dim(proj_grads, core * half_width, half_width, 1)
    give = lax.dynamic_slice_in_dim(proj_grads, (1 - core) * half_width, half_width, 1)
    own = ordered(core, mine, lax.ppermute(give, "dp", core_swap), 0)

    by_part = lax.ppermute(own, "dp", part_swap)
    by_side = lax.ppermute(own, "dp", side_swap)
    near = lax.ppermute(own, "dp", near_swap)
    first_part = jnp.dot(proj_grads, val_grads, preferred_element_type=jnp.float32)
    first_local = first_part + lax.ppermute(first_part, "feat", feat_swap)

    own_late, by_part_late, first_local = lax.optimization_barrier((own, by_part, first_local))
    far = lax.ppermute(own_late, "dp", far_move)
    by_both = lax.ppermute(by_part_late, "dp", side_swap)
    half = lax.axis_size("dp") // 2
    first_half = lax.all_gather(
        first_local, "dp", axis=0, tiled=True,
        axis_index_groups=[list(range(half)), list(range(half, 2 * half))],
    )

    def summed(tile):
        rows = tile.shape[0] // 2
        keep = lax.dynamic_slice_in_dim(tile, core * rows, rows, 0)
        send = lax.dynamic_slice_in_dim(tile, (1 - core) * rows, rows, 0)
        tile = keep + lax.ppermute(send, "dp", core_swap)
        rows = rows // 2
        keep = lax.dynamic_slice_in_dim(tile, feat_index * rows, rows, 0)
        send = lax.dynamic_slice_in_dim(tile, (1 - feat_index) * rows, rows, 0)
        return keep + lax.ppermute(send, "feat", feat_swap)

    rows_a = jnp.where(is_inner, near, own)
    early = summed(
        jnp.concatenate([pair_tile(rows_a, cols) for cols in (own, by_side, by_part)], 1)
    )
    far, by_both, early, first_half = lax.optimization_barrier((far, by_both, early, first_half))
    rows_b = jnp.where(is_inner, far, by_part)
    late_b = summed(
        jnp.concatenate([pair_tile(rows_b, cols) for cols in (own, by_side, by_part, by_both)], 1)
    )
    late_a = summed(pair_tile(rows_a, by_both))
    gram = jnp.concatenate([jnp.concatenate([early, late_a], 1), late_b], 0)

    chip_cols = own.shape[0]
    own_x, side_x, part_x, both_x = (
        gram[:, i * chip_cols:(i + 1) * chip_cols] for i in range(4)
    )
    gram_cols = ordered(
        part % 2,
        ordered(side, own_x, side_x, 1),
        ordered(side, part_x, both_x, 1),
        1,
    )
    rows_of = jnp.asarray(ROWS_OF, jnp.int32)[part]
    piece = row_count // 2
    row_base = ((rows_of * 2 + side) * 2 + core) * row_count + feat_index * piece
    row_ids = (row_base[:, None] + jnp.arange(piece, dtype=jnp.int32)[None, :]).reshape(-1)
    col_count = gram_cols.shape[1]
    col_ids = (part // 2) * col_count + jnp.arange(col_count, dtype=jnp.int32)
    pair_values = jnp.where(row_ids[:, None] == col_ids[None, :], 0.0, gram_cols)
    rounded, pair_values = lax.optimization_barrier(
        (pair_values.astype(jnp.bfloat16), pair_values)
    )
    partial_sum = jnp.dot(pair_values, first_half, precision=lax.Precision.HIGHEST)

    def deliver(values):
        out = []
        for flip in (0, 1):
            sent = jnp.where((feat_index ^ flip) == 0, values[:piece], values[piece:])
            out.append(lax.ppermute(sent, both, [
                (at(p, s, c) * 2 + f, at(ROWS_OF[p][f ^ flip], s, c) * 2 + p // 2)
                for p in range(4) for s in (0, 1) for c in (0, 1) for f in (0, 1)
            ]))
        return ordered((part + feat_index) % 2, out[0], out[1], 0)

    interactions = deliver(rounded)
    half_sum = deliver(partial_sum)
    pair_sum = half_sum + lax.ppermute(half_sum, "feat", feat_swap)
    return (interactions, first_local - pair_weight * pair_sum)


def solution(mesh):
    split = mesh.shape["feat"] == 2 and mesh.shape["dp"] == 16
    return jax.shard_map(
        split_body if split else general_body,
        mesh=mesh,
        in_specs=(P("dp", "feat"), P("feat", None)),
        out_specs=(P("dp", "feat"), P("dp", None)),
        check_vma=False,
    )
```
